256 devices in a mesh: rep: 16 (over x, z_lo, core), tp: 16 (over y, z_hi).
Axes of the slice: x: 4, y: 4, z: 8 (z_hi: 4, z_lo: 2; z = z_hi * 2 + z_lo), core: 2. Of those that a mesh axis runs over, the one named last changes fastest.
Arguments:
- acts: bfloat16 [6144, 8192], P('rep', 'tp'), may hold values from -6 to 6
- base_weight: bfloat16 [8192, 8192], P('tp'), may hold values from -0.0625 to 0.0625
- a_high: bfloat16 [32, 128, 8192], P('rep', None, 'tp'), may hold values from -0.0625 to 0.0625
- b_high: bfloat16 [32, 128, 8192], P('rep', None, 'tp'), may hold values from -0.5 to 0.5
- a_mid: bfloat16 [64, 32, 8192], P('rep', None, 'tp'), may hold values from -0.0625 to 0.0625
- b_mid: bfloat16 [64, 32, 8192], P('rep', None, 'tp'), may hold values from -1 to 1
- a_low: bfloat16 [128, 8, 8192], P('rep', None, 'tp'), may hold values from -0.0625 to 0.0625
- b_low: bfloat16 [128, 8, 8192], P('rep', None, 'tp'), may hold values from -2 to 2
- row_adapter: int32 [6144], P('rep'), may hold values from 0 to 223
- home_high: int32 [32], replicated, may hold values from 0 to 31, each once
- home_mid: int32 [64], replicated, may hold values from 0 to 63, each once
- home_low: int32 [128], replicated, may hold values from 0 to 127, each once
Outputs:
- projected: bfloat16 [6144, 8192], P('rep', 'tp')
The draws below stay inside these ranges and needn't reach their ends.
All inputs are finite; a program needn't handle non-finite values.
Results may differ from the reference program's by a relative error of at most 0.0039.
Values may be sent and summed in bfloat16 or wider, within the bound.
A program may use at most 128 MiB of HBM per device.

```python
import math
import jax
import jax.numpy as jnp
import numpy as np

D = 8192
R_HIGH = 128
R_MID = 32
R_LOW = 8
HIGH_ALL = 32
MID_ALL = 64
LOW_ALL = 128
ADAPTERS = 224
ROWS_ALL = 6144


def with_ends(entries, stream_key, least, top_value):
    dims = entries.shape
    spot = [jax.random.randint(jax.random.fold_in(stream_key, axis), (), 0, dims[axis]) for axis in range(len(dims))]
    entries = entries.at[tuple(spot)].set(least)
    longest = dims.index(max(dims))
    spot[longest] = (spot[longest] + 1) % dims[longest]
    return entries.at[tuple(spot)].set(top_value)


def block_scale(rng, dims, cuts, smallest, largest):
    loudness = 1.0
    for axis_at, blocks in cuts:
        steps = jax.random.uniform(jax.random.fold_in(jax.random.fold_in(rng, 6), axis_at), (blocks,), jnp.float32, smallest / len(cuts), largest / len(cuts))
        loudness = loudness * jnp.repeat(jnp.exp(steps), dims[axis_at] // blocks).reshape((-1,) + (1,) * (len(dims) - 1 - axis_at))
    return loudness


def cumulative_ranks(count, lean):
    portions = [(1 << 20) // math.isqrt(grade ** lean) + 1 for grade in range(1, count + 1)]
    scale = 1 + sum(portions) // (1 << 30)
    return np.cumsum(np.array([max(1, weight // scale) for weight in portions]))


def skewed_ids(own_key, dims, number_of, skew):
    table = cumulative_ranks(number_of, skew)
    pick = jax.random.randint(jax.random.fold_in(own_key, 1), dims, 0, int(table[number_of - 1]))
    grade = jnp.searchsorted(jnp.asarray(table, jnp.int32), pick, side="right")
    return jax.random.permutation(jax.random.fold_in(own_key, 2), number_of)[grade].astype(jnp.int32)


def centred(stream_key, dims, deviation, bound, pieces=(), kind=jnp.bfloat16):
    array = jax.random.normal(stream_key, dims, jnp.float32) * deviation
    if len(pieces) > 0:
        array = block_scale(stream_key, dims, pieces, -0.22, 0.18) * array
    return jnp.clip(array, min=-bound, max=bound).astype(kind)


def setup_inputs(seed: int = 0) -> dict:
    splits = jax.random.split(jax.random.key(seed), 13)
    return {
        "acts": centred(splits[0], (ROWS_ALL, D), 1.0, 6.0, ((0, 16), (1, 16))),
        "base_weight": centred(splits[1], (D, D), D ** -0.5, 0.0625, ((0, 16),)),
        "a_high": centred(splits[2], (HIGH_ALL, R_HIGH, D), D ** -0.5, 0.0625, ((0, 16), (2, 16))),
        "b_high": centred(splits[3], (HIGH_ALL, R_HIGH, D), R_HIGH ** -0.5, 0.5, ((0, 16), (2, 16))),
        "a_mid": centred(splits[4], (MID_ALL, R_MID, D), D ** -0.5, 0.0625, ((0, 16), (2, 16))),
        "b_mid": centred(splits[5], (MID_ALL, R_MID, D), R_MID ** -0.5, 1.0, ((0, 16), (2, 16))),
        "a_low": centred(splits[6], (LOW_ALL, R_LOW, D), D ** -0.5, 0.0625, ((0, 16), (2, 16))),
        "b_low": centred(splits[7], (LOW_ALL, R_LOW, D), R_LOW ** -0.5, 2.0, ((0, 16), (2, 16))),
        "row_adapter": with_ends(skewed_ids(splits[8], (ROWS_ALL,), ADAPTERS, 2), jax.random.fold_in(splits[8], 3), 0, ADAPTERS - 1).astype(jnp.int32),
        "home_high": jax.random.permutation(splits[9], HIGH_ALL).astype(jnp.int32),
        "home_mid": jax.random.permutation(splits[10], MID_ALL).astype(jnp.int32),
        "home_low": jax.random.permutation(splits[11], LOW_ALL).astype(jnp.int32),
    }


def store_rows(ids, home, offset):
    local = ids - offset
    count = home.shape[0]
    match = local[:, None] == jnp.arange(count, dtype=jnp.int32)[None, :]
    return jnp.sum(jnp.where(match, home[None, :] + 1, 0), axis=1).astype(jnp.int32) - 1


def bucket_delta(acts, store_a, store_b, rows_k):
    count, rank, width = store_a.shape
    total = acts.shape[0]
    flat_a = store_a.reshape(count * rank, width)
    products = jnp.dot(acts, flat_a.T, preferred_element_type=jnp.float32)
    chosen = rows_k[:, None] == jnp.arange(count, dtype=jnp.int32)[None, :]
    shrink = jnp.sum(products.reshape(total, count, rank) * chosen[:, :, None], axis=1).astype(jnp.bfloat16)
    spread = jnp.where(chosen[:, :, None], shrink[:, None, :], jnp.zeros((), jnp.bfloat16)).reshape(total, count * rank)
    return jnp.dot(spread, store_b.reshape(count * rank, width), preferred_element_type=jnp.float32)


def reference(acts, base_weight, a_high, b_high, a_mid, b_mid, a_low, b_low, row_adapter, home_high, home_mid, home_low):
    base = jnp.dot(acts, base_weight, preferred_element_type=jnp.float32)
    high_count = home_high.shape[0]
    mid_count = home_mid.shape[0]
    delta = bucket_delta(acts, a_high, b_high, store_rows(row_adapter, home_high, 0))
    delta = delta + bucket_delta(acts, a_mid, b_mid, store_rows(row_adapter, home_mid, high_count))
    delta = delta + bucket_delta(acts, a_low, b_low, store_rows(row_adapter, home_low, high_count + mid_count))
    return (base + delta).astype(jnp.bfloat16)
```

```python
import functools

import jax
import jax.numpy as jnp
from jax import lax
from jax.experimental import pallas as pl
from jax.experimental.pallas import tpu as pltpu
from jax.sharding import PartitionSpec as P

F32 = jnp.float32
BF16 = jnp.bfloat16
MESH = pl.DeviceIdType.MESH
ROWS = 384
HALF = 192
COLS = 512
PART = 256
RANKS = 448
PAIR = 2 * RANKS
LANES = 128
OPP, NEXT, PREV, OWN = range(4)
STEP = (2, 1, 3, 0)
TILES = ((OPP, 0), (OPP, 1), (NEXT, 1), (PREV, 0), (NEXT, 0), (PREV, 1), (OWN, 0), (OWN, 1))
AHEAD = 2


def dot(a, b):
    return jnp.dot(a, b, preferred_element_type=F32)


def dot_nt(a, b):
    return lax.dot_general(a, b, (((1,), (1,)), ((), ())), preferred_element_type=F32)


def pair_codes(pair):
    lane = lax.broadcasted_iota(jnp.int32, (1, LANES), 1).astype(F32)
    mid = jnp.floor(lane * (1.0 / 32.0))
    low = jnp.floor(lane * (1.0 / 8.0))
    none = jnp.zeros_like(lane)
    return (
        none + 4.0 * pair,
        none + (4.0 * pair + 1.0),
        mid + (16.0 + 8.0 * pair),
        low + (48.0 + 16.0 * pair),
        none + (4.0 * pair + 2.0),
        none + (4.0 * pair + 3.0),
        mid + (20.0 + 8.0 * pair),
    )


def kernel(
    acts,
    weight,
    a_high,
    a_mid,
    a_low,
    b_high,
    b_mid,
    b_low,
    ids,
    home_high,
    home_mid,
    home_low,
    out,
    xs,
    wb,
    a_all,
    b_all,
    ids_all,
    codes,
    m_send,
    m_recv,
    z_send,
    z_recv,
    own_sum,
    shr,
    shr_y,
    shr_z,
    shr_sum,
    shr_b,
    delta,
    delta_send,
    delta_recv,
    spread,
    local_sems,
    send_sems,
    recv_sems,
):
    rep = lax.axis_index("rep")
    tp = lax.axis_index("tp")
    x, z_lo, core = rep // 4, lax.rem(rep // 2, 2), lax.rem(rep, 2)
    y, z_hi = tp // 4, lax.rem(tp, 4)

    def peer(dx=0, dy=0, dz=0, flip_z=0, flip_core=0):
        to_rep = (
            lax.rem(x + dx, 4) * 4
            + lax.rem(z_lo + flip_z, 2) * 2
            + lax.rem(core + flip_core, 2)
        )
        return (to_rep, lax.rem(y + dy, 4) * 4 + lax.rem(z_hi + dz, 4))

    y_next, y_prev, y_opp = peer(dy=1), peer(dy=3), peer(dy=2)
    z_next, z_prev, z_opp = peer(dz=1), peer(dz=3), peer(dz=2)
    x_next, x_prev = peer(dx=1), peer(dx=3)
    mate, other = peer(flip_core=1), peer(flip_z=1)
    peers = (y_next, y_prev, y_opp, z_next, z_prev, z_opp, x_next, x_prev, mate, other)

    n_local = [0]

    def fetch(src, dst):
        copy = pltpu.make_async_copy(src, dst, local_sems.at[n_local[0]])
        n_local[0] += 1
        copy.start()
        return copy

    sent = []

    def send(src, dst, to):
        copy = pltpu.make_async_remote_copy(
            src_ref=src,
            dst_ref=dst,
            send_sem=send_sems.at[len(sent)],
            recv_sem=recv_sems.at[len(sent)],
            device_id=to,
            device_id_type=MESH,
        )
        copy.start()
        sent.append(copy)
        return copy

    barrier = pltpu.get_barrier_semaphore()
    for to in peers:
        pl.semaphore_signal(barrier, inc=1, device_id=to, device_id_type=MESH)

    got_x = fetch(acts, xs.at[pl.ds(0, ROWS)])

    def fetch_weight(group, place):
        block = lax.rem(y + STEP[place], 4) * 4 + lax.rem(z_hi + STEP[group], 4)
        start = pl.multiple_of(block * COLS, COLS)
        return fetch(weight.at[:, pl.ds(start, COLS)], wb.at[group, place])

    got_w = {}
    for place in range(4):
        got_w[OPP, place] = fetch_weight(OPP, place)
    got_a = (
        fetch(a_high, a_all.at[0, pl.ds(0, 256)]),
        fetch(a_mid, a_all.at[0, pl.ds(256, 128)]),
        fetch(a_low, a_all.at[0, pl.ds(384, 64)]),
    )
    got_ids = fetch(ids, ids_all.at[0])
    for group in (NEXT, PREV, OWN):
        for place in range(4):
            got_w[group, place] = fetch_weight(group, place)
    got_b = (
        fetch(b_high, b_all.at[0, pl.ds(0, 256)]),
        fetch(b_mid, b_all.at[0, pl.ds(256, 128)]),
        fetch(b_low, b_all.at[0, pl.ds(384, 64)]),
    )

    def rows_of(t):
        return xs[pl.ds(TILES[t][1] * HALF, HALF), :]

    def w_of(t, place):
        return wb.at[TILES[t][0], place]

    LEFT, RIGHT = pl.ds(0, PART), pl.ds(PART, PART)
    arrive = {}

    def first(t):
        if (TILES[t][0], OPP) in got_w:
            for place in range(4):
                got_w.pop((TILES[t][0], place)).wait()
        rows = rows_of(t)
        far = dot(rows, w_of(t, OPP)[...]).astype(BF16)
        m_send[t, 0] = far[:, :PART]
        m_send[t, 1] = far[:, PART:]
        m_send[t, 2] = dot(rows, w_of(t, NEXT)[:, RIGHT]).astype(BF16)
        m_send[t, 3] = dot(rows, w_of(t, PREV)[:, LEFT]).astype(BF16)

    def first_send(t):
        for k, to in ((0, y_next), (1, y_prev), (2, y_next), (3, y_prev)):
            arrive[t, k] = send(m_send.at[t, k], m_recv.at[t, k], to)

    def second(t):
        rows = rows_of(t)
        arrive[t, 0].wait_recv()
        near = dot(rows, w_of(t, NEXT)[:, LEFT])
        m_send[t, 4] = (near + m_recv[t, 0].astype(F32)).astype(BF16)
        arrive[t, 4] = send(m_send.at[t, 4], m_recv.at[t, 4], y_next)
        arrive[t, 1].wait_recv()
        near = dot(rows, w_of(t, PREV)[:, RIGHT])
        m_send[t, 5] = (near + m_recv[t, 1].astype(F32)).astype(BF16)
        arrive[t, 5] = send(m_send.at[t, 5], m_recv.at[t, 5], y_prev)

    z_arrive = {}
    Z_PLACE = (z_next, z_prev, z_next, z_prev, z_next, z_prev)

    def third(t):
        group, half = TILES[t]
        own = dot(rows_of(t), w_of(t, OWN)[...])
        for k in (2, 3, 4, 5):
            arrive[t, k].wait_recv()
        left = own[:, :PART] + (m_recv[t, 4].astype(F32) + m_recv[t, 3].astype(F32))
        right = own[:, PART:] + (m_recv[t, 5].astype(F32) + m_recv[t, 2].astype(F32))
        if t in (4, 5):
            z_arrive[t - 4].wait_recv()
            left = left + z_recv[t - 4, :, LEFT].astype(F32)
            right = right + z_recv[t - 4, :, RIGHT].astype(F32)
        if group == OWN:
            own_sum[pl.ds(half * HALF, HALF), LEFT] = left
            own_sum[pl.ds(half * HALF, HALF), RIGHT] = right
        else:
            z_send[t, :, LEFT] = left.astype(BF16)
            z_send[t, :, RIGHT] = right.astype(BF16)
            z_arrive[t] = send(z_send.at[t], z_recv.at[t], Z_PLACE[t])

    def spread_own(store, landed):
        landed["next"] = send(store.at[0, pl.ds(0, RANKS)], store.at[PREV, pl.ds(0, RANKS)], x_next)
        landed["prev"] = send(store.at[0, pl.ds(0, RANKS)], store.at[NEXT, pl.ds(0, RANKS)], x_prev)

    def to_mate(store, landed, pair):
        landed[pair] = (
            send(store.at[pair, pl.ds(0, 384)], store.at[pair, pl.ds(512, 384)], mate),
            send(store.at[pair, pl.ds(384, 64)], store.at[pair, pl.ds(448, 64)], mate),
        )

    def forward(store, landed):
        half = RANKS // 2
        landed["next"].wait_recv()
        landed["far_next"] = send(
            store.at[PREV, pl.ds(0, half)], store.at[3, pl.ds(0, half)], x_next
        )
        landed["prev"].wait_recv()
        landed["far_prev"] = send(
            store.at[NEXT, pl.ds(half, half)], store.at[3, pl.ds(half, half)], x_prev
        )
        to_mate(store, landed, PREV)
        to_mate(store, landed, NEXT)

    def forward_far(store, landed):
        landed["far_next"].wait_recv()
        landed["far_prev"].wait_recv()
        to_mate(store, landed, 3)

    def wait_pair(landed, pair):
        for copy in landed[pair]:
            copy.wait_recv()

    def number_rows():
        def place(owner):
            owner_x = owner // 4
            away = lax.rem(owner_x - x + 4, 4)
            slot = jnp.where(away == 0, 0, jnp.where(away == 1, NEXT, jnp.where(away == 3, PREV, 3)))
            same = lax.rem(owner // 2, 2) == z_lo
            return same, slot * 2 + lax.rem(lax.rem(owner, 2) + core, 2)

        def numbers(home, each, base):
            store = home[...]
            same, slot = place(store // each)
            return jnp.where(same, base + slot * each + lax.rem(store, each) + 1, 0).astype(F32)

        tables = (
            numbers(home_high, 2, 0),
            numbers(home_mid, 4, 16),
            numbers(home_low, 8, 48),
        )
        offsets = (0.0, 32.0, 96.0)
        eye = lax.broadcasted_iota(jnp.int32, (LANES, LANES), 0) == lax.broadcasted_iota(
            jnp.int32, (LANES, LANES), 1
        )
        for part in range(2):
            for block in range(3):
                row_ids = ids_all[part, pl.ds(block, 1), :].astype(F32)
                column = jnp.sum(jnp.where(eye, row_ids, 0.0), axis=1, keepdims=True)
                found = jnp.zeros((LANES, 1), F32)
                for table, offset in zip(tables, offsets):
                    lane = lax.broadcasted_iota(jnp.int32, (1, table.shape[1]), 1).astype(F32)
                    hit = column == lane + offset
                    found = found + jnp.sum(jnp.where(hit, table, 0.0), axis=1, keepdims=True)
                start = part * ROWS + block * LANES
                codes[pl.ds(start, LANES), :] = jnp.broadcast_to(found - 1.0, (LANES, LANES))

    def shrink(pair):
        wait_pair(landed_a, pair)
        tiles = pair_codes(pair)

        @pl.loop(0, 2)
        def _(part):
            rows = pl.ds(pl.multiple_of(part * ROWS, ROWS), ROWS)
            products = dot_nt(xs[rows, :], a_all[pair])
            code = codes[rows, :]
            total = jnp.zeros((ROWS, LANES), F32) if pair == 0 else shr[rows, :]
            for k, tile in enumerate(tiles):
                total = total + jnp.where(code == tile, products[:, k * LANES : (k + 1) * LANES], 0.0)
            shr[rows, :] = total

    SHR_Y, SHR_Z = 192, 48

    def shrink_y():
        for k, (step, to) in enumerate(((1, y_next), (3, y_prev), (2, y_opp))):
            start = pl.multiple_of(lax.rem(y + step, 4) * SHR_Y, SHR_Y)
            z_arrive["y", k] = send(shr.at[pl.ds(start, SHR_Y)], shr_y.at[k], to)

    def shrink_z():
        for k in range(3):
            z_arrive["y", k].wait_recv()
        start = pl.multiple_of(y * SHR_Y, SHR_Y)
        shr_sum[...] = (shr[pl.ds(start, SHR_Y), :] + shr_y[0]) + (shr_y[1] + shr_y[2])
        for k, (step, to) in enumerate(((1, z_next), (3, z_prev), (2, z_opp))):
            start = pl.multiple_of(lax.rem(z_hi + step, 4) * SHR_Z, SHR_Z)
            z_arrive["z", k] = send(shr_sum.at[pl.ds(start, SHR_Z)], shr_z.at[k], to)

    def gather_z():
        for k in range(3):
            z_arrive["z", k].wait_recv()
        start = pl.multiple_of(z_hi * SHR_Z, SHR_Z)
        total = (shr_sum[pl.ds(start, SHR_Z), :] + shr_z[0]) + (shr_z[1] + shr_z[2])
        mine = pl.ds(pl.multiple_of(y * SHR_Y + z_hi * SHR_Z, SHR_Z), SHR_Z)
        shr_b[mine, :] = total.astype(BF16)
        for k, to in enumerate((z_next, z_prev, z_opp)):
            z_arrive["gz", k] = send(shr_b.at[mine], shr_b.at[mine], to)

    def gather_y():
        for k in range(3):
            z_arrive["gz", k].wait_recv()
        mine = pl.ds(pl.multiple_of(y * SHR_Y, SHR_Y), SHR_Y)
        for k, to in enumerate((y_next, y_prev, y_opp)):
            z_arrive["gy", k] = send(shr_b.at[mine], shr_b.at[mine], to)

    def spread_rows(part):
        if part == 1:
            for k in range(3):
                z_arrive["gy", k].wait_recv()
        rows = pl.ds(part * ROWS, ROWS)
        code = codes[rows, :]
        value = shr_b[rows, :].astype(F32)
        for pair in range(4):
            for k, tile in enumerate(pair_codes(pair)):
                lanes = pl.ds(pair * PAIR + k * LANES, LANES)
                spread[:, lanes] = jnp.where(code == tile, value, 0.0).astype(BF16)

    def expand(part):
        spread_rows(part)
        total = dot(spread[...], b_all[...].reshape(4 * PAIR, COLS))
        if part == 1:
            delta_send[...] = total.astype(BF16)
            z_arrive["delta"] = send(delta_send, delta_recv, other)
        else:
            delta[...] = total

    def finish():
        z_arrive["delta"].wait_recv()
        for half in range(2):
            rows = pl.ds(half * HALF, HALF)
            near, far = (4, 3) if half == 0 else (5, 2)
            z_arrive[near].wait_recv()
            z_arrive[far].wait_recv()
            base = own_sum[rows, :] + (z_recv[near].astype(F32) + z_recv[far].astype(F32))
            out[rows, :] = (base + (delta[rows, :] + delta_recv[rows, :].astype(F32))).astype(BF16)

    landed_a, landed_b = {}, {}
    got_x.wait()
    first(0)
    pl.semaphore_wait(barrier, len(peers))
    first_send(0)
    for copy in got_a:
        copy.wait()
    spread_own(a_all, landed_a)
    to_mate(a_all, landed_a, 0)
    x_other = send(xs.at[pl.ds(0, ROWS)], xs.at[pl.ds(ROWS, ROWS)], other)
    got_ids.wait()
    ids_other = send(ids_all.at[0], ids_all.at[1], other)
    first(1)
    first_send(1)
    second(0)
    first(2)
    first_send(2)
    second(1)
    third(0)
    forward(a_all, landed_a)
    ids_other.wait_recv()
    number_rows()
    first(3)
    first_send(3)
    second(2)
    third(1)
    x_other.wait_recv()
    shrink(0)
    for copy in got_b:
        copy.wait()
    spread_own(b_all, landed_b)
    to_mate(b_all, landed_b, 0)
    forward_far(a_all, landed_a)
    shrink(NEXT)
    first(4)
    first_send(4)
    second(3)
    shrink(PREV)
    third(2)
    shrink(3)
    shrink_y()
    first(5)
    first_send(5)
    second(4)
    third(3)
    shrink_z()
    forward(b_all, landed_b)
    first(6)
    first_send(6)
    second(5)
    gather_z()
    third(4)
    first(7)
    first_send(7)
    gather_y()
    second(6)
    forward_far(b_all, landed_b)
    third(5)
    second(7)
    for pair in (0, NEXT, PREV, 3):
        wait_pair(landed_b, pair)
    expand(1)
    expand(0)
    third(6)
    third(7)
    finish()
    for copy in sent:
        copy.wait_send()


N_LOCAL = 24
N_REMOTE = 100


def shards(
    acts,
    base_weight,
    a_high,
    b_high,
    a_mid,
    b_mid,
    a_low,
    b_low,
    row_adapter,
    home_high,
    home_mid,
    home_low,
):
    anywhere = pl.BlockSpec(memory_space=pl.ANY)
    vmem = pl.BlockSpec(memory_space=pltpu.VMEM)
    return pl.pallas_call(
        kernel,
        out_shape=jax.ShapeDtypeStruct((ROWS, COLS), BF16),
        in_specs=[anywhere] * 9 + [vmem] * 3,
        out_specs=vmem,
        scratch_shapes=[
            pltpu.VMEM((2 * ROWS, COLS), BF16),
            pltpu.VMEM((4, 4, COLS, COLS), BF16),
            pltpu.VMEM((4, PAIR, COLS), BF16),
            pltpu.VMEM((4, PAIR, COLS), BF16),
            pltpu.VMEM((2, 3, LANES), jnp.int32),
            pltpu.VMEM((2 * ROWS, LANES), F32),
            pltpu.VMEM((8, 6, HALF, PART), BF16),
            pltpu.VMEM((8, 6, HALF, PART), BF16),
            pltpu.VMEM((6, HALF, COLS), BF16),
            pltpu.VMEM((6, HALF, COLS), BF16),
            pltpu.VMEM((ROWS, COLS), F32),
            pltpu.VMEM((2 * ROWS, LANES), F32),
            pltpu.VMEM((3, 192, LANES), F32),
            pltpu.VMEM((3, 48, LANES), F32),
            pltpu.VMEM((192, LANES), F32),
            pltpu.VMEM((2 * ROWS, LANES), BF16),
            pltpu.VMEM((ROWS, COLS), F32),
            pltpu.VMEM((ROWS, COLS), BF16),
            pltpu.VMEM((ROWS, COLS), BF16),
            pltpu.VMEM((ROWS, 4 * PAIR), BF16),
            pltpu.SemaphoreType.DMA((N_LOCAL,)),
            pltpu.SemaphoreType.DMA((N_REMOTE,)),
            pltpu.SemaphoreType.DMA((N_REMOTE,)),
        ],
        compiler_params=pltpu.CompilerParams(
            collective_id=0, has_side_effects=True, vmem_limit_bytes=58 * 2**20
        ),
        cost_estimate=pl.CostEstimate(
            flops=9_000_000_000, bytes_accessed=16_000_000, transcendentals=0
        ),
        name="project",
    )(
        acts,
        base_weight,
        a_high.reshape(256, COLS),
        a_mid.reshape(128, COLS),
        a_low.reshape(64, COLS),
        b_high.reshape(256, COLS),
        b_mid.reshape(128, COLS),
        b_low.reshape(64, COLS),
        row_adapter.reshape(3, LANES),
        home_high.reshape(1, 32),
        home_mid.reshape(1, 64),
        home_low.reshape(1, 128),
    )


def solution(mesh):
    return jax.shard_map(
        shards,
        mesh=mesh,
        in_specs=(
            P("rep", "tp"),
            P("tp", None),
            P("rep", None, "tp"),
            P("rep", None, "tp"),
            P("rep", None, "tp"),
            P("rep", None, "tp"),
            P("rep", None, "tp"),
            P("rep", None, "tp"),
            P("rep"),
            P(),
            P(),
            P(),
        ),
        out_specs=P("rep", "tp"),
        check_vma=False,
    )
```

```python
import functools

import jax
import jax.numpy as jnp
from jax import lax
from jax.experimental import pallas as pl
from jax.experimental.pallas import tpu as pltpu
from jax.sharding import PartitionSpec as P

F32 = jnp.float32
BF16 = jnp.bfloat16
MESH = pl.DeviceIdType.MESH
ROWS = 384
TALL = 96
SHR_Y, SHR_Z = 96, 24
PIECE = 224
COLS = 512
PART = 256
RANKS = 448
PAIR = 2 * RANKS
LANES = 128
OPP, NEXT, PREV, OWN = range(4)
STEP = (2, 1, 3, 0)
TILES = (
    ((OPP, 0), (OPP, 2), (OPP, 1), (OPP, 3))
    + ((NEXT, 2), (PREV, 0), (NEXT, 3), (PREV, 1))
    + ((NEXT, 0), (PREV, 2), (NEXT, 1), (PREV, 3))
    + ((OWN, 0), (OWN, 2), (OWN, 1), (OWN, 3))
)
TO_NEXT = {(OPP, 0), (OPP, 1), (NEXT, 0), (NEXT, 1), (NEXT, 2), (NEXT, 3)}


def dot(a, b):
    return jnp.dot(a, b, preferred_element_type=F32)


def dot_nt(a, b):
    return lax.dot_general(a, b, (((1,), (1,)), ((), ())), preferred_element_type=F32)


def pair_codes(pair):
    lane = lax.broadcasted_iota(jnp.int32, (1, LANES), 1).astype(F32)
    mid = jnp.floor(lane * (1.0 / 32.0))
    low = jnp.floor(lane * (1.0 / 8.0))
    none = jnp.zeros_like(lane)
    return (
        none + 4.0 * pair,
        none + (4.0 * pair + 1.0),
        mid + (16.0 + 8.0 * pair),
        low + (48.0 + 16.0 * pair),
        none + (4.0 * pair + 2.0),
        none + (4.0 * pair + 3.0),
        mid + (20.0 + 8.0 * pair),
    )


def kernel(
    acts,
    weight,
    a_high,
    a_mid,
    a_low,
    b_high,
    b_mid,
    b_low,
    ids,
    home_high,
    home_mid,
    home_low,
    out,
    xs,
    wb,
    a_all,
    b_all,
    ids_all,
    codes,
    codes_other,
    m_send,
    m_recv,
    z_send,
    z_recv,
    own_sum,
    shr,
    shr_part,
    shr_y,
    shr_z,
    shr_sum,
    shr_round,
    shr_b,
    delta,
    local_sems,
    send_sems,
    recv_sems,
):
    rep = lax.axis_index("rep")
    tp = lax.axis_index("tp")
    x, z_lo, core = rep // 4, lax.rem(rep // 2, 2), lax.rem(rep, 2)
    y, z_hi = tp // 4, lax.rem(tp, 4)

    def peer(dx=0, dy=0, dz=0, flip_z=0, flip_core=0):
        to_rep = (
            lax.rem(x + dx, 4) * 4
            + lax.rem(z_lo + flip_z, 2) * 2
            + lax.rem(core + flip_core, 2)
        )
        return (to_rep, lax.rem(y + dy, 4) * 4 + lax.rem(z_hi + dz, 4))

    y_next, y_prev = peer(dy=1), peer(dy=3)
    z_next, z_prev = peer(dz=1), peer(dz=3)
    x_next, x_prev = peer(dx=1), peer(dx=3)
    mate, other = peer(flip_core=1), peer(flip_z=1)
    y_opp, z_opp = peer(dy=2), peer(dz=2)
    peers = (y_next, y_prev, y_opp, z_next, z_prev, z_opp, x_next, x_prev, mate, other)

    n_local = [0]

    def fetch(src, dst):
        copy = pltpu.make_async_copy(src, dst, local_sems.at[n_local[0]])
        n_local[0] += 1
        copy.start()
        return copy

    sent = []

    def send(src, dst, to):
        copy = pltpu.make_async_remote_copy(
            src_ref=src,
            dst_ref=dst,
            send_sem=send_sems.at[len(sent)],
            recv_sem=recv_sems.at[len(sent)],
            device_id=to,
            device_id_type=MESH,
        )
        copy.start()
        sent.append(copy)
        return copy

    barrier = pltpu.get_barrier_semaphore()
    for to in peers:
        pl.semaphore_signal(barrier, inc=1, device_id=to, device_id_type=MESH)

    got_x = fetch(acts, xs.at[pl.ds(0, ROWS)])

    def fetch_weight(group, place):
        block = lax.rem(y + STEP[place], 4) * 4 + lax.rem(z_hi + STEP[group], 4)
        start = pl.multiple_of(block * COLS, COLS)
        return fetch(weight.at[:, pl.ds(start, COLS)], wb.at[group, place])

    got_w = {}
    for place in range(4):
        got_w[OPP, place] = fetch_weight(OPP, place)
    got_a = (
        fetch(a_high, a_all.at[0, pl.ds(0, 256)]),
        fetch(a_mid, a_all.at[0, pl.ds(256, 128)]),
        fetch(a_low, a_all.at[0, pl.ds(384, 64)]),
    )
    got_ids = fetch(ids, ids_all.at[0])
    for group in (NEXT, PREV, OWN):
        for place in range(4):
            got_w[group, place] = fetch_weight(group, place)
    got_b = (
        fetch(b_high, b_all.at[0, pl.ds(0, 256)]),
        fetch(b_mid, b_all.at[0, pl.ds(256, 128)]),
        fetch(b_low, b_all.at[0, pl.ds(384, 64)]),
    )

    def rows_of(t):
        return xs[pl.ds(TILES[t][1] * TALL, TALL), :]

    def w_of(t, place):
        return wb.at[TILES[t][0], place]

    LEFT, RIGHT = pl.ds(0, PART), pl.ds(PART, PART)
    arrive = {}

    def across(t, k):
        to = y_next if k % 2 == 0 else y_prev
        arrive[t, k] = send(m_send.at[t, k], m_recv.at[t, k], to)

    def first(t):
        if (TILES[t][0], OPP) in got_w:
            for place in range(4):
                got_w.pop((TILES[t][0], place)).wait()
        far = dot(rows_of(t), w_of(t, OPP)[...]).astype(BF16)
        m_send[t, 0] = far[:, :PART]
        m_send[t, 1] = far[:, PART:]

    def first_send(t):
        across(t, 0)
        across(t, 1)

    def direct(t):
        rows = rows_of(t)
        m_send[t, 2] = dot(rows, w_of(t, NEXT)[:, RIGHT]).astype(BF16)
        across(t, 2)
        m_send[t, 3] = dot(rows, w_of(t, PREV)[:, LEFT]).astype(BF16)
        across(t, 3)

    def second(t):
        rows = rows_of(t)
        for k, place, cols in ((0, NEXT, LEFT), (1, PREV, RIGHT)):
            arrive[t, k].wait_recv()
            near = dot(rows, w_of(t, place)[:, cols])
            m_send[t, k + 4] = (near + m_recv[t, k].astype(F32)).astype(BF16)
            across(t, k + 4)

    z_arrive = {}

    def third(t):
        group, quarter = TILES[t]
        own = dot(rows_of(t), w_of(t, OWN)[...])
        for k in (2, 3, 4, 5):
            arrive[t, k].wait_recv()
        left = own[:, :PART] + (m_recv[t, 4].astype(F32) + m_recv[t, 3].astype(F32))
        right = own[:, PART:] + (m_recv[t, 5].astype(F32) + m_recv[t, 2].astype(F32))
        if 8 <= t < 12:
            z_arrive[t - 8].wait_recv()
            left = left + z_recv[t - 8, :, LEFT].astype(F32)
            right = right + z_recv[t - 8, :, RIGHT].astype(F32)
        if group == OWN:
            own_sum[pl.ds(quarter * TALL, TALL), LEFT] = left
            own_sum[pl.ds(quarter * TALL, TALL), RIGHT] = right
        else:
            z_send[t, :, LEFT] = left.astype(BF16)
            z_send[t, :, RIGHT] = right.astype(BF16)
            to = z_next if TILES[t] in TO_NEXT else z_prev
            z_arrive[t] = send(z_send.at[t], z_recv.at[t], to)

    def spread_own(store, landed, n, base=0):
        low, high = pl.ds(0, PIECE), pl.ds(PIECE, PIECE)
        ahead, behind = (low, high) if n == 0 else (high, low)
        landed["next", n] = send(store.at[base, ahead], store.at[base + PREV, ahead], x_next)
        landed["prev", n] = send(store.at[base, behind], store.at[base + NEXT, behind], x_prev)

    def to_mate(store, landed, pair, base=0):
        block = base + pair
        landed[pair] = (
            send(store.at[block, pl.ds(0, 384)], store.at[block, pl.ds(512, 384)], mate),
            send(store.at[block, pl.ds(384, 64)], store.at[block, pl.ds(448, 64)], mate),
        )

    def forward(store, landed, base=0):
        low, high = pl.ds(0, PIECE), pl.ds(PIECE, PIECE)
        landed["next", 0].wait_recv()
        landed["far_next"] = send(store.at[base + PREV, low], store.at[base + 3, low], x_next)
        landed["prev", 0].wait_recv()
        landed["far_prev"] = send(store.at[base + NEXT, high], store.at[base + 3, high], x_prev)

    def forward_near(store, landed, base=0):
        landed["next", 1].wait_recv()
        to_mate(store, landed, PREV, base)
        landed["prev", 1].wait_recv()
        to_mate(store, landed, NEXT, base)

    def forward_far(store, landed, base=0):
        landed["far_next"].wait_recv()
        landed["far_prev"].wait_recv()
        to_mate(store, landed, 3, base)

    def wait_pair(landed, pair):
        for copy in landed[pair]:
            copy.wait_recv()

    def number_rows():
        def place(owner):
            owner_x = owner // 4
            away = lax.rem(owner_x - x + 4, 4)
            slot = jnp.where(away == 0, 0, jnp.where(away == 1, NEXT, jnp.where(away == 3, PREV, 3)))
            same = lax.rem(owner // 2, 2) == z_lo
            return same.astype(jnp.int32), slot * 2 + lax.rem(lax.rem(owner, 2) + core, 2)

        def numbers(home, each, base):
            store = home[...]
            same, slot = place(store // each)
            number = base + slot * each + lax.rem(store, each) + 1
            return tuple(jnp.where(same == k, number, 0).astype(F32) for k in (1, 0))

        tables = (
            numbers(home_high, 2, 0),
            numbers(home_mid, 4, 16),
            numbers(home_low, 8, 48),
        )
        offsets = (0.0, 32.0, 96.0)
        eye = lax.broadcasted_iota(jnp.int32, (LANES, LANES), 0) == lax.broadcasted_iota(
            jnp.int32, (LANES, LANES), 1
        )
        for part in range(2):
            for block in range(3):
                row_ids = ids_all[part, pl.ds(block, 1), :].astype(F32)
                column = jnp.sum(jnp.where(eye, row_ids, 0.0), axis=1, keepdims=True)
                start = part * ROWS + block * LANES
                for side, store in ((0, codes), (1, codes_other))[: 2 - part]:
                    found = jnp.zeros((LANES, 1), F32)
                    for table, offset in zip(tables, offsets):
                        lane = lax.broadcasted_iota(jnp.int32, (1, table[side].shape[1]), 1)
                        hit = column == lane.astype(F32) + offset
                        found = found + jnp.sum(
                            jnp.where(hit, table[side], 0.0), axis=1, keepdims=True
                        )
                    store[pl.ds(start, LANES), :] = jnp.broadcast_to(found - 1.0, (LANES, LANES))

    def shrink(pair):
        wait_pair(landed_a, pair)
        tiles = pair_codes(pair)

        @pl.loop(0, 2)
        def _(part):
            rows = pl.ds(pl.multiple_of(part * ROWS, ROWS), ROWS)
            products = dot_nt(xs[rows, :], a_all[pair])
            code = codes[rows, :]
            total = jnp.zeros((ROWS, LANES), F32) if pair == 0 else shr[rows, :]
            for k, tile in enumerate(tiles):
                total = total + jnp.where(code == tile, products[:, k * LANES : (k + 1) * LANES], 0.0)
            shr[rows, :] = total

    AWAY = (1, 3, 2)
    Y_TEAM, Z_TEAM = (y_next, y_prev, y_opp), (z_next, z_prev, z_opp)

    def part_of(index, size):
        return pl.ds(pl.multiple_of(lax.rem(index, 4) * size, size), size)

    def shrink_other():
        z_arrive["other"] = send(shr.at[pl.ds(ROWS, ROWS)], shr_part, other)

    def shrink_y():
        z_arrive["other"].wait_recv()
        shr_part[...] += shr[pl.ds(0, ROWS), :]
        for k in range(3):
            z_arrive["y", k] = send(shr_part.at[part_of(y + AWAY[k], SHR_Y)], shr_y.at[k], Y_TEAM[k])

    def shrink_z():
        for k in range(3):
            z_arrive["y", k].wait_recv()
        shr_sum[...] = (shr_part[part_of(y, SHR_Y), :] + shr_y[0]) + (shr_y[1] + shr_y[2])
        for k in range(3):
            z_arrive["z", k] = send(
                shr_sum.at[part_of(z_hi + AWAY[k], SHR_Z)], shr_z.at[k], Z_TEAM[k]
            )

    def gather_z():
        for k in range(3):
            z_arrive["z", k].wait_recv()
        mine = part_of(z_hi, SHR_Z)
        total = (shr_sum[mine, :] + shr_z[0]) + (shr_z[1] + shr_z[2])
        shr_round[mine, :] = total.astype(BF16).astype(F32)
        for k in range(3):
            z_arrive["gz", k] = send(shr_round.at[mine], shr_round.at[mine], Z_TEAM[k])

    def gather_y():
        for k in range(3):
            z_arrive["gz", k].wait_recv()
        mine = part_of(y, SHR_Y)
        shr_b[mine, :] = shr_round[...].astype(BF16)
        for k in range(3):
            z_arrive["gy", k] = send(shr_b.at[mine], shr_b.at[mine], Y_TEAM[k])

    def wait_shrink():
        for k in range(3):
            z_arrive["gy", k].wait_recv()

    def expand(side):
        landed, code = ((landed_b, codes), (landed_c, codes_other))[side]
        for pair in (0, NEXT, PREV, 3):
            wait_pair(landed, pair)
        code = code[pl.ds(0, ROWS), :].astype(BF16)
        value = shr_b[...]
        none = jnp.zeros_like(value)
        total = delta[...] if side else None
        for pair in range(4):
            tiles = pair_codes(pair)
            piece = jnp.concatenate(
                [jnp.where(code == tile.astype(BF16), value, none) for tile in tiles], axis=1
            )
            part = dot(piece, b_all[side * 4 + pair])
            total = part if total is None else total + part
        delta[...] = total

    def finish():
        for quarter, (near, far) in enumerate(((8, 5), (10, 7), (9, 4), (11, 6))):
            z_arrive[near].wait_recv()
            z_arrive[far].wait_recv()
            rows = pl.ds(quarter * TALL, TALL)
            add = z_recv[near].astype(F32) + z_recv[far].astype(F32)
            out[rows, :] = ((own_sum[rows, :] + add) + delta[rows, :]).astype(BF16)

    landed_a, landed_b, landed_c = {}, {}, {}
    got_x.wait()
    first(0)
    pl.semaphore_wait(barrier, len(peers))
    first_send(0)
    direct(0)
    for copy in got_a:
        copy.wait()
    spread_own(a_all, landed_a, 0)
    spread_own(a_all, landed_a, 1)
    to_mate(a_all, landed_a, 0)
    x_other = send(xs.at[pl.ds(0, ROWS)], xs.at[pl.ds(ROWS, ROWS)], other)
    got_ids.wait()
    ids_other = send(ids_all.at[0], ids_all.at[1], other)
    first(1)
    first_send(1)
    direct(1)
    first(2)
    first_send(2)
    direct(2)
    first(3)
    first_send(3)
    second(0)
    first(4)
    first_send(4)
    direct(3)
    for copy in got_b:
        copy.wait()
    b_other = send(b_all.at[0, pl.ds(0, RANKS)], b_all.at[4, pl.ds(0, RANKS)], other)
    second(1)
    first(5)
    first_send(5)
    direct(4)
    forward(a_all, landed_a)
    spread_own(b_all, landed_b, 0)
    spread_own(b_all, landed_b, 1)
    to_mate(b_all, landed_b, 0)
    second(2)
    first(6)
    first_send(6)
    direct(5)
    second(3)
    first(7)
    first_send(7)
    direct(6)
    second(4)
    first(8)
    first_send(8)
    third(0)
    direct(7)
    forward_near(a_all, landed_a)
    ids_other.wait_recv()
    number_rows()
    x_other.wait_recv()
    second(5)
    first(9)
    first_send(9)
    third(1)
    direct(8)
    shrink(0)
    shrink(1)
    second(6)
    first(10)
    first_send(10)
    third(2)
    direct(9)
    b_other.wait_recv()
    spread_own(b_all, landed_c, 0, 4)
    spread_own(b_all, landed_c, 1, 4)
    to_mate(b_all, landed_c, 0, 4)
    shrink(2)
    forward_far(a_all, landed_a)
    shrink(3)
    shrink_other()
    second(7)
    first(11)
    first_send(11)
    third(3)
    direct(10)
    second(8)
    first(12)
    first_send(12)
    third(4)
    direct(11)
    forward(b_all, landed_b)
    second(9)
    first(13)
    first_send(13)
    third(5)
    direct(12)
    shrink_y()
    forward_near(b_all, landed_b)
    second(10)
    first(14)
    first_send(14)
    third(6)
    direct(13)
    second(11)
    first(15)
    first_send(15)
    third(7)
    direct(14)
    shrink_z()
    forward(b_all, landed_c, 4)
    second(12)
    third(8)
    direct(15)
    gather_z()
    forward_near(b_all, landed_c, 4)
    second(13)
    third(9)
    gather_y()
    forward_far(b_all, landed_b)
    second(14)
    third(10)
    forward_far(b_all, landed_c, 4)
    second(15)
    third(11)
    wait_shrink()
    expand(0)
    expand(1)
    third(12)
    third(13)
    third(14)
    third(15)
    finish()
    for copy in sent:
        copy.wait_send()


N_LOCAL = 24
N_REMOTE = 200


def shards(
    acts,
    base_weight,
    a_high,
    b_high,
    a_mid,
    b_mid,
    a_low,
    b_low,
    row_adapter,
    home_high,
    home_mid,
    home_low,
):
    anywhere = pl.BlockSpec(memory_space=pl.ANY)
    vmem = pl.BlockSpec(memory_space=pltpu.VMEM)
    return pl.pallas_call(
        kernel,
        out_shape=jax.ShapeDtypeStruct((ROWS, COLS), BF16),
        in_specs=[anywhere] * 9 + [vmem] * 3,
        out_specs=vmem,
        scratch_shapes=[
            pltpu.VMEM((2 * ROWS, COLS), BF16),
            pltpu.VMEM((4, 4, COLS, COLS), BF16),
            pltpu.VMEM((4, PAIR, COLS), BF16),
            pltpu.VMEM((8, PAIR, COLS), BF16),
            pltpu.VMEM((2, 3, LANES), jnp.int32),
            pltpu.VMEM((2 * ROWS, LANES), F32),
            pltpu.VMEM((ROWS, LANES), F32),
            pltpu.VMEM((16, 6, TALL, PART), BF16),
            pltpu.VMEM((16, 6, TALL, PART), BF16),
            pltpu.VMEM((12, TALL, COLS), BF16),
            pltpu.VMEM((12, TALL, COLS), BF16),
            pltpu.VMEM((ROWS, COLS), F32),
            pltpu.VMEM((2 * ROWS, LANES), F32),
            pltpu.VMEM((ROWS, LANES), F32),
            pltpu.VMEM((3, SHR_Y, LANES), F32),
            pltpu.VMEM((3, SHR_Z, LANES), F32),
            pltpu.VMEM((SHR_Y, LANES), F32),
            pltpu.VMEM((SHR_Y, LANES), F32),
            pltpu.VMEM((ROWS, LANES), BF16),
            pltpu.VMEM((ROWS, COLS), F32),
            pltpu.SemaphoreType.DMA((N_LOCAL,)),
            pltpu.SemaphoreType.DMA((N_REMOTE,)),
            pltpu.SemaphoreType.DMA((N_REMOTE,)),
        ],
        compiler_params=pltpu.CompilerParams(
            collective_id=0, has_side_effects=True, vmem_limit_bytes=58 * 2**20
        ),
        cost_estimate=pl.CostEstimate(
            flops=9_000_000_000, bytes_accessed=16_000_000, transcendentals=0
        ),
        name="project",
    )(
        acts,
        base_weight,
        a_high.reshape(256, COLS),
        a_mid.reshape(128, COLS),
        a_low.reshape(64, COLS),
        b_high.reshape(256, COLS),
        b_mid.reshape(128, COLS),
        b_low.reshape(64, COLS),
        row_adapter.reshape(3, LANES),
        home_high.reshape(1, 32),
        home_mid.reshape(1, 64),
        home_low.reshape(1, 128),
    )


def solution(mesh):
    return jax.shard_map(
        shards,
        mesh=mesh,
        in_specs=(
            P("rep", "tp"),
            P("tp", None),
            P("rep", None, "tp"),
            P("rep", None, "tp"),
            P("rep", None, "tp"),
            P("rep", None, "tp"),
            P("rep", None, "tp"),
            P("rep", None, "tp"),
            P("rep"),
            P(),
            P(),
            P(),
        ),
        out_specs=P("rep", "tp"),
        check_vma=False,
    )
```

```python
import functools

import jax
import jax.numpy as jnp
from jax import lax
from jax.experimental import pallas as pl
from jax.experimental.pallas import tpu as pltpu
from jax.sharding import PartitionSpec as P

F32 = jnp.float32
BF16 = jnp.bfloat16
MESH = pl.DeviceIdType.MESH
ROWS = 384
TALL = 96
SHR_Y, SHR_Z = 96, 24
PIECE = 224
COLS = 512
PART = 256
RANKS = 448
PAIR = 2 * RANKS
LANES = 128
OPP, NEXT, PREV, OWN = range(4)
STEP = (2, 1, 3, 0)
TILES = (
    ((OPP, 0), (OPP, 2), (OPP, 1), (OPP, 3))
    + ((NEXT, 2), (PREV, 0), (NEXT, 3), (PREV, 1))
    + ((NEXT, 0), (PREV, 2), (NEXT, 1), (PREV, 3))
    + ((OWN, 0), (OWN, 2), (OWN, 1), (OWN, 3))
)
TO_NEXT = {(OPP, 0), (OPP, 1), (NEXT, 0), (NEXT, 1), (NEXT, 2), (NEXT, 3)}


def dot(a, b):
    return jnp.dot(a, b, preferred_element_type=F32)


def dot_nt(a, b):
    return lax.dot_general(a, b, (((1,), (1,)), ((), ())), preferred_element_type=F32)


def pair_codes(pair):
    lane = lax.broadcasted_iota(jnp.int32, (1, LANES), 1).astype(F32)
    mid = jnp.floor(lane * (1.0 / 32.0))
    low = jnp.floor(lane * (1.0 / 8.0))
    none = jnp.zeros_like(lane)
    return (
        none + 4.0 * pair,
        none + (4.0 * pair + 1.0),
        mid + (16.0 + 8.0 * pair),
        low + (48.0 + 16.0 * pair),
        none + (4.0 * pair + 2.0),
        none + (4.0 * pair + 3.0),
        mid + (20.0 + 8.0 * pair),
    )


def kernel(
    acts,
    weight,
    a_high,
    a_mid,
    a_low,
    b_high,
    b_mid,
    b_low,
    ids,
    home_high,
    home_mid,
    home_low,
    out,
    xs,
    wb,
    a_all,
    b_all,
    ids_all,
    codes,
    codes_other,
    m_send,
    m_recv,
    z_send,
    z_recv,
    own_sum,
    shr,
    shr_part,
    shr_y,
    shr_z,
    shr_sum,
    shr_round,
    shr_b,
    delta,
    local_sems,
    send_sems,
    recv_sems,
):
    rep = lax.axis_index("rep")
    tp = lax.axis_index("tp")
    x, z_lo, core = rep // 4, lax.rem(rep // 2, 2), lax.rem(rep, 2)
    y, z_hi = tp // 4, lax.rem(tp, 4)

    def peer(dx=0, dy=0, dz=0, flip_z=0, flip_core=0):
        to_rep = (
            lax.rem(x + dx, 4) * 4
            + lax.rem(z_lo + flip_z, 2) * 2
            + lax.rem(core + flip_core, 2)
        )
        return (to_rep, lax.rem(y + dy, 4) * 4 + lax.rem(z_hi + dz, 4))

    y_next, y_prev = peer(dy=1), peer(dy=3)
    z_next, z_prev = peer(dz=1), peer(dz=3)
    x_next, x_prev = peer(dx=1), peer(dx=3)
    mate, other = peer(flip_core=1), peer(flip_z=1)
    y_opp, z_opp = peer(dy=2), peer(dz=2)
    peers = (y_next, y_prev, y_opp, z_next, z_prev, z_opp, x_next, x_prev, mate, other)

    n_local = [0]

    def fetch(src, dst):
        copy = pltpu.make_async_copy(src, dst, local_sems.at[n_local[0]])
        n_local[0] += 1
        copy.start()
        return copy

    sent = []

    def send(src, dst, to):
        copy = pltpu.make_async_remote_copy(
            src_ref=src,
            dst_ref=dst,
            send_sem=send_sems.at[len(sent)],
            recv_sem=recv_sems.at[len(sent)],
            device_id=to,
            device_id_type=MESH,
        )
        copy.start()
        sent.append(copy)
        return copy

    barrier = pltpu.get_barrier_semaphore()
    for to in peers:
        pl.semaphore_signal(barrier, inc=1, device_id=to, device_id_type=MESH)

    got_x = fetch(acts, xs.at[pl.ds(0, ROWS)])

    def fetch_weight(group, place):
        block = lax.rem(y + STEP[place], 4) * 4 + lax.rem(z_hi + STEP[group], 4)
        start = pl.multiple_of(block * COLS, COLS)
        return fetch(weight.at[:, pl.ds(start, COLS)], wb.at[group, place])

    got_w = {}
    for place in range(4):
        got_w[OPP, place] = fetch_weight(OPP, place)
    got_a = (
        fetch(a_high, a_all.at[0, pl.ds(0, 256)]),
        fetch(a_mid, a_all.at[0, pl.ds(256, 128)]),
        fetch(a_low, a_all.at[0, pl.ds(384, 64)]),
    )
    got_ids = fetch(ids, ids_all.at[0])
    for group in (NEXT, PREV, OWN):
        for place in range(4):
            got_w[group, place] = fetch_weight(group, place)
    got_b = (
        fetch(b_high, b_all.at[0, pl.ds(0, 256)]),
        fetch(b_mid, b_all.at[0, pl.ds(256, 128)]),
        fetch(b_low, b_all.at[0, pl.ds(384, 64)]),
    )

    def rows_of(t):
        return xs[pl.ds(TILES[t][1] * TALL, TALL), :]

    def w_of(t, place):
        return wb.at[TILES[t][0], place]

    LEFT, RIGHT = pl.ds(0, PART), pl.ds(PART, PART)
    arrive = {}

    def across(t, k):
        to = y_next if k % 2 == 0 else y_prev
        arrive[t, k] = send(m_send.at[t, k], m_recv.at[t, k], to)

    def first(t):
        if (TILES[t][0], OPP) in got_w:
            for place in range(4):
                got_w.pop((TILES[t][0], place)).wait()
        far = dot(rows_of(t), w_of(t, OPP)[...]).astype(BF16)
        m_send[t, 0] = far[:, :PART]
        m_send[t, 1] = far[:, PART:]

    def first_send(t):
        across(t, 0)
        across(t, 1)

    def direct(t):
        rows = rows_of(t)
        m_send[t, 2] = dot(rows, w_of(t, NEXT)[:, RIGHT]).astype(BF16)
        across(t, 2)
        m_send[t, 3] = dot(rows, w_of(t, PREV)[:, LEFT]).astype(BF16)
        across(t, 3)

    def second(t):
        rows = rows_of(t)
        for k, place, cols in ((0, NEXT, LEFT), (1, PREV, RIGHT)):
            arrive[t, k].wait_recv()
            near = dot(rows, w_of(t, place)[:, cols])
            m_send[t, k + 4] = (near + m_recv[t, k].astype(F32)).astype(BF16)
            across(t, k + 4)

    z_arrive = {}

    def third(t):
        group, quarter = TILES[t]
        own = dot(rows_of(t), w_of(t, OWN)[...])
        for k in (2, 3, 4, 5):
            arrive[t, k].wait_recv()
        left = own[:, :PART] + (m_recv[t, 4].astype(F32) + m_recv[t, 3].astype(F32))
        right = own[:, PART:] + (m_recv[t, 5].astype(F32) + m_recv[t, 2].astype(F32))
        if 8 <= t < 12:
            z_arrive[t - 8].wait_recv()
            left = left + z_recv[t - 8, :, LEFT].astype(F32)
            right = right + z_recv[t - 8, :, RIGHT].astype(F32)
        if group == OWN:
            own_sum[pl.ds(quarter * TALL, TALL), LEFT] = left
            own_sum[pl.ds(quarter * TALL, TALL), RIGHT] = right
        else:
            z_send[t, :, LEFT] = left.astype(BF16)
            z_send[t, :, RIGHT] = right.astype(BF16)
            to = z_next if TILES[t] in TO_NEXT else z_prev
            z_arrive[t] = send(z_send.at[t], z_recv.at[t], to)

    def spread_own(store, landed, n, base=0):
        low, high = pl.ds(0, PIECE), pl.ds(PIECE, PIECE)
        ahead, behind = (low, high) if n == 0 else (high, low)
        landed["next", n] = send(store.at[base, ahead], store.at[base + PREV, ahead], x_next)
        landed["prev", n] = send(store.at[base, behind], store.at[base + NEXT, behind], x_prev)

    def to_mate(store, landed, pair, base=0):
        block = base + pair
        landed[pair] = (
            send(store.at[block, pl.ds(0, 384)], store.at[block, pl.ds(512, 384)], mate),
            send(store.at[block, pl.ds(384, 64)], store.at[block, pl.ds(448, 64)], mate),
        )

    def forward(store, landed, base=0):
        low, high = pl.ds(0, PIECE), pl.ds(PIECE, PIECE)
        landed["next", 0].wait_recv()
        landed["far_next"] = send(store.at[base + PREV, low], store.at[base + 3, low], x_next)
        landed["prev", 0].wait_recv()
        landed["far_prev"] = send(store.at[base + NEXT, high], store.at[base + 3, high], x_prev)

    def forward_near(store, landed, base=0):
        landed["next", 1].wait_recv()
        to_mate(store, landed, PREV, base)
        landed["prev", 1].wait_recv()
        to_mate(store, landed, NEXT, base)

    def forward_far(store, landed, base=0):
        landed["far_next"].wait_recv()
        landed["far_prev"].wait_recv()
        to_mate(store, landed, 3, base)

    def wait_pair(landed, pair):
        for copy in landed[pair]:
            copy.wait_recv()

    def number_rows():
        def place(owner):
            owner_x = owner // 4
            away = lax.rem(owner_x - x + 4, 4)
            slot = jnp.where(away == 0, 0, jnp.where(away == 1, NEXT, jnp.where(away == 3, PREV, 3)))
            same = lax.rem(owner // 2, 2) == z_lo
            return same.astype(jnp.int32), slot * 2 + lax.rem(lax.rem(owner, 2) + core, 2)

        def numbers(home, each, base):
            store = home[...]
            same, slot = place(store // each)
            number = base + slot * each + lax.rem(store, each) + 1
            return tuple(jnp.where(same == k, number, 0).astype(F32) for k in (1, 0))

        tables = (
            numbers(home_high, 2, 0),
            numbers(home_mid, 4, 16),
            numbers(home_low, 8, 48),
        )
        offsets = (0.0, 32.0, 96.0)
        eye = lax.broadcasted_iota(jnp.int32, (LANES, LANES), 0) == lax.broadcasted_iota(
            jnp.int32, (LANES, LANES), 1
        )
        for part in range(2):
            for block in range(3):
                row_ids = ids_all[part, pl.ds(block, 1), :].astype(F32)
                column = jnp.sum(jnp.where(eye, row_ids, 0.0), axis=1, keepdims=True)
                start = part * ROWS + block * LANES
                for side, store in ((0, codes), (1, codes_other))[: 2 - part]:
                    found = jnp.zeros((LANES, 1), F32)
                    for table, offset in zip(tables, offsets):
                        lane = lax.broadcasted_iota(jnp.int32, (1, table[side].shape[1]), 1)
                        hit = column == lane.astype(F32) + offset
                        found = found + jnp.sum(
                            jnp.where(hit, table[side], 0.0), axis=1, keepdims=True
                        )
                    store[pl.ds(start, LANES), :] = jnp.broadcast_to(found - 1.0, (LANES, LANES))

    def shrink(pair):
        wait_pair(landed_a, pair)
        tiles = pair_codes(pair)

        @pl.loop(0, 2)
        def _(part):
            rows = pl.ds(pl.multiple_of(part * ROWS, ROWS), ROWS)
            products = dot_nt(xs[rows, :], a_all[pair])
            code = codes[rows, :]
            total = jnp.zeros((ROWS, LANES), F32) if pair == 0 else shr[rows, :]
            for k, tile in enumerate(tiles):
                total = total + jnp.where(code == tile, products[:, k * LANES : (k + 1) * LANES], 0.0)
            shr[rows, :] = total

    AWAY = (1, 3, 2)
    Y_TEAM, Z_TEAM = (y_next, y_prev, y_opp), (z_next, z_prev, z_opp)

    def part_of(index, size):
        return pl.ds(pl.multiple_of(lax.rem(index, 4) * size, size), size)

    def shrink_other():
        z_arrive["other"] = send(shr.at[pl.ds(ROWS, ROWS)], shr_part, other)

    def shrink_y():
        z_arrive["other"].wait_recv()
        shr_part[...] += shr[pl.ds(0, ROWS), :]
        for k in range(3):
            z_arrive["y", k] = send(shr_part.at[part_of(y + AWAY[k], SHR_Y)], shr_y.at[k], Y_TEAM[k])

    def shrink_z():
        for k in range(3):
            z_arrive["y", k].wait_recv()
        shr_sum[...] = (shr_part[part_of(y, SHR_Y), :] + shr_y[0]) + (shr_y[1] + shr_y[2])
        for k in range(3):
            z_arrive["z", k] = send(
                shr_sum.at[part_of(z_hi + AWAY[k], SHR_Z)], shr_z.at[k], Z_TEAM[k]
            )

    def gather_z():
        for k in range(3):
            z_arrive["z", k].wait_recv()
        mine = part_of(z_hi, SHR_Z)
        total = (shr_sum[mine, :] + shr_z[0]) + (shr_z[1] + shr_z[2])
        shr_round[mine, :] = total.astype(BF16).astype(F32)
        for k in range(3):
            z_arrive["gz", k] = send(shr_round.at[mine], shr_round.at[mine], Z_TEAM[k])

    def gather_y():
        for k in range(3):
            z_arrive["gz", k].wait_recv()
        mine = part_of(y, SHR_Y)
        shr_b[mine, :] = shr_round[...].astype(BF16)
        for k in range(3):
            z_arrive["gy", k] = send(shr_b.at[mine], shr_b.at[mine], Y_TEAM[k])

    def wait_shrink():
        for k in range(3):
            z_arrive["gy", k].wait_recv()

    def expand(side):
        landed, code = ((landed_b, codes), (landed_c, codes_other))[side]
        for pair in (0, NEXT, PREV, 3):
            wait_pair(landed, pair)
        code = code[pl.ds(0, ROWS), :].astype(BF16)
        value = shr_b[...]
        none = jnp.zeros_like(value)
        total = delta[...] if side else None
        for pair in range(4):
            tiles = pair_codes(pair)
            piece = jnp.concatenate(
                [jnp.where(code == tile.astype(BF16), value, none) for tile in tiles], axis=1
            )
            part = dot(piece, b_all[side * 4 + pair])
            total = part if total is None else total + part
        delta[...] = total

    def finish():
        for quarter, (near, far) in enumerate(((8, 5), (10, 7), (9, 4), (11, 6))):
            z_arrive[near].wait_recv()
            z_arrive[far].wait_recv()
            rows = pl.ds(quarter * TALL, TALL)
            add = z_recv[near].astype(F32) + z_recv[far].astype(F32)
            out[rows, :] = ((own_sum[rows, :] + add) + delta[rows, :]).astype(BF16)

    landed_a, landed_b, landed_c = {}, {}, {}
    got_x.wait()
    first(0)
    pl.semaphore_wait(barrier, len(peers))
    first_send(0)
    direct(0)
    for copy in got_a:
        copy.wait()
    spread_own(a_all, landed_a, 0)
    spread_own(a_all, landed_a, 1)
    to_mate(a_all, landed_a, 0)
    x_other = send(xs.at[pl.ds(0, ROWS)], xs.at[pl.ds(ROWS, ROWS)], other)
    got_ids.wait()
    ids_other = send(ids_all.at[0], ids_all.at[1], other)
    first(1)
    first_send(1)
    direct(1)
    first(2)
    first_send(2)
    direct(2)
    first(3)
    first_send(3)
    second(0)
    first(4)
    first_send(4)
    direct(3)
    for copy in got_b:
        copy.wait()
    b_other = send(b_all.at[0, pl.ds(0, RANKS)], b_all.at[4, pl.ds(0, RANKS)], other)
    second(1)
    first(5)
    first_send(5)
    direct(4)
    forward(a_all, landed_a)
    spread_own(b_all, landed_b, 0)
    spread_own(b_all, landed_b, 1)
    to_mate(b_all, landed_b, 0)
    second(2)
    first(6)
    first_send(6)
    direct(5)
    second(3)
    first(7)
    first_send(7)
    third(0)
    direct(6)
    second(4)
    first(8)
    first_send(8)
    third(1)
    direct(7)
    forward_near(a_all, landed_a)
    ids_other.wait_recv()
    number_rows()
    x_other.wait_recv()
    second(5)
    first(9)
    first_send(9)
    third(2)
    direct(8)
    shrink(0)
    shrink(1)
    second(6)
    first(10)
    first_send(10)
    third(3)
    direct(9)
    b_other.wait_recv()
    spread_own(b_all, landed_c, 0, 4)
    spread_own(b_all, landed_c, 1, 4)
    to_mate(b_all, landed_c, 0, 4)
    shrink(2)
    forward_far(a_all, landed_a)
    shrink(3)
    shrink_other()
    second(7)
    first(11)
    first_send(11)
    third(4)
    direct(10)
    second(8)
    first(12)
    first_send(12)
    third(5)
    direct(11)
    forward(b_all, landed_b)
    second(9)
    first(13)
    first_send(13)
    third(6)
    direct(12)
    shrink_y()
    forward_near(b_all, landed_b)
    second(10)
    first(14)
    first_send(14)
    third(7)
    direct(13)
    second(11)
    first(15)
    first_send(15)
    third(8)
    direct(14)
    shrink_z()
    forward(b_all, landed_c, 4)
    second(12)
    third(9)
    direct(15)
    gather_z()
    forward_near(b_all, landed_c, 4)
    second(13)
    third(10)
    gather_y()
    forward_far(b_all, landed_b)
    second(14)
    third(11)
    forward_far(b_all, landed_c, 4)
    second(15)
    third(12)
    third(13)
    third(14)
    wait_shrink()
    expand(0)
    expand(1)
    third(15)
    finish()
    for copy in sent:
        copy.wait_send()


N_LOCAL = 24
N_REMOTE = 200


def shards(
    acts,
    base_weight,
    a_high,
    b_high,
    a_mid,
    b_mid,
    a_low,
    b_low,
    row_adapter,
    home_high,
    home_mid,
    home_low,
):
    anywhere = pl.BlockSpec(memory_space=pl.ANY)
    vmem = pl.BlockSpec(memory_space=pltpu.VMEM)
    return pl.pallas_call(
        kernel,
        out_shape=jax.ShapeDtypeStruct((ROWS, COLS), BF16),
        in_specs=[anywhere] * 9 + [vmem] * 3,
        out_specs=vmem,
        scratch_shapes=[
            pltpu.VMEM((2 * ROWS, COLS), BF16),
            pltpu.VMEM((4, 4, COLS, COLS), BF16),
            pltpu.VMEM((4, PAIR, COLS), BF16),
            pltpu.VMEM((8, PAIR, COLS), BF16),
            pltpu.VMEM((2, 3, LANES), jnp.int32),
            pltpu.VMEM((2 * ROWS, LANES), F32),
            pltpu.VMEM((ROWS, LANES), F32),
            pltpu.VMEM((16, 6, TALL, PART), BF16),
            pltpu.VMEM((16, 6, TALL, PART), BF16),
            pltpu.VMEM((12, TALL, COLS), BF16),
            pltpu.VMEM((12, TALL, COLS), BF16),
            pltpu.VMEM((ROWS, COLS), F32),
            pltpu.VMEM((2 * ROWS, LANES), F32),
            pltpu.VMEM((ROWS, LANES), F32),
            pltpu.VMEM((3, SHR_Y, LANES), F32),
            pltpu.VMEM((3, SHR_Z, LANES), F32),
            pltpu.VMEM((SHR_Y, LANES), F32),
            pltpu.VMEM((SHR_Y, LANES), F32),
            pltpu.VMEM((ROWS, LANES), BF16),
            pltpu.VMEM((ROWS, COLS), F32),
            pltpu.SemaphoreType.DMA((N_LOCAL,)),
            pltpu.SemaphoreType.DMA((N_REMOTE,)),
            pltpu.SemaphoreType.DMA((N_REMOTE,)),
        ],
        compiler_params=pltpu.CompilerParams(
            collective_id=0, has_side_effects=True, vmem_limit_bytes=58 * 2**20
        ),
        cost_estimate=pl.CostEstimate(
            flops=9_000_000_000, bytes_accessed=16_000_000, transcendentals=0
        ),
        name="project",
    )(
        acts,
        base_weight,
        a_high.reshape(256, COLS),
        a_mid.reshape(128, COLS),
        a_low.reshape(64, COLS),
        b_high.reshape(256, COLS),
        b_mid.reshape(128, COLS),
        b_low.reshape(64, COLS),
        row_adapter.reshape(3, LANES),
        home_high.reshape(1, 32),
        home_mid.reshape(1, 64),
        home_low.reshape(1, 128),
    )


def solution(mesh):
    return jax.shard_map(
        shards,
        mesh=mesh,
        in_specs=(
            P("rep", "tp"),
            P("tp", None),
            P("rep", None, "tp"),
            P("rep", None, "tp"),
            P("rep", None, "tp"),
            P("rep", None, "tp"),
            P("rep", None, "tp"),
            P("rep", None, "tp"),
            P("rep"),
            P(),
            P(),
            P(),
        ),
        out_specs=P("rep", "tp"),
        check_vma=False,
    )
```
